32 devices in a mesh: groups: 2 (over y), tensor: 16 (over z, x, core).
Axes of the slice: x: 2, y: 2, z: 4, core: 2. Of those that a mesh axis runs over, the one named last changes fastest.
Arguments:
- output_gradient: bfloat16 [384, 8192], P(('groups', 'tensor')), parts along dimension 0, may hold values from -6 to 6
- hidden: bfloat16 [384, 29568], P('groups', 'tensor'), parts along dimension 0, may hold values from -6 to 6
- down_matrix: bfloat16 [29568, 8192], P('tensor'), may hold values from -0.03125 to 0.03125
- first_adapter_factor: bfloat16 [32, 29568, 64], P('groups', 'tensor'), parts along dimension 0, may hold values from -0.03125 to 0.03125
- second_adapter_factor: bfloat16 [32, 64, 8192], P(('groups', 'tensor')), parts along dimension 0, may hold values from -0.75 to 0.75
- counts: int32 [32], P('groups'), parts along dimension 0, may hold values from 1 to 36, 192 in all
- adapter_slots: int32 [32], P('groups'), parts along dimension 0, may hold values from 0 to 15, each once
Outputs:
- hidden_gradient: bfloat16 [384, 29568], P('groups', 'tensor'), parts along dimension 0
- second_factor_gradient: float32 [32, 64, 8192], P(('groups', 'tensor')), parts along dimension 0
The draws below stay inside these ranges and needn't reach their ends.
There are 2 independent parts, one for each index of `groups`. The reference program is written for one: setup_inputs(seed, part) draws one part's arguments, and reference() takes and returns one part's arrays. A program takes and returns all parts, laid end to end along the dimension named above; an argument that names none is the same for every part. Nothing has to cross between parts.
Inputs may be any that keep to these rules, and one draw needn't show every extreme that they name: `counts`: every adapter has at least one token, one adapter has exactly 36. `adapter_slots`: each slot holds exactly one adapter.
All inputs are finite; a program needn't handle non-finite values.
Results may differ from the reference program's by a relative error of at most 0.0046.
Values may be sent and summed in bfloat16 or wider, within the bound.
A program may use at most 192 MiB of HBM per device.

```python
import math
import jax
import jax.numpy as jnp
import numpy as np
from jax import lax

MODEL_DIM = 8192
HIDDEN_UNITS = 29568
ADAPTER_RANK = 64
ADAPTER_COUNT = 16
TOKENS = 192
MAX_TOKENS = 36


def steps_of(stream_key, dims, split, least, high):
    loudness, own = 1.0, jax.random.fold_in(stream_key, 6)
    for position, shards_of in split:
        draws = jnp.exp(jax.random.uniform(jax.random.fold_in(own, position), (shards_of,), jnp.float32, least / len(split), high / len(split)))
        loudness = loudness * jnp.repeat(draws, dims[position] // shards_of).reshape([-1 if axis == position else 1 for axis in range(len(dims))])
    return loudness


def length_profile(count, total, bound, lean):
    loads = [(1 << 20) // math.isqrt(rank ** lean) + 1 for rank in range(2, count + 1)]
    surplus, given = total - bound - (count - 1), [1] * (count - 1)
    while surplus > 0:
        candidates = [i for i in range(count - 1) if given[i] < bound]
        whole, budget = sum([loads[i] for i in candidates]), surplus
        for i in candidates:
            extra = min(bound - given[i], max(1, budget * loads[i] // whole), surplus)
            given[i] = given[i] + extra
            surplus = surplus - extra
    return np.array([bound] + given)


def ragged_sizes(stream_key, count, total, most, lean):
    if count == 2:
        one = jax.random.randint(stream_key, (), max(1, total - most), min(most, total - 1) + 1)
        return jnp.stack([one, total - one])
    lengths = jnp.asarray(length_profile(count, total, most, lean), jnp.int32)
    twos = (count - 1) // 2
    source_of, receiver = lengths[1:1 + 2 * twos:2], lengths[2:2 + 2 * twos:2]
    room = jnp.minimum(source_of - 1, most - receiver)
    moved = jax.random.randint(jax.random.fold_in(stream_key, 1), (twos,), 0, 1 << 20) % (room + 1)
    lengths = lengths.at[1:1 + 2 * twos:2].set(source_of - moved).at[2:2 + 2 * twos:2].set(receiver + moved)
    return lengths[jax.random.permutation(jax.random.fold_in(stream_key, 2), count)]


def normal_values(own_key, extent, deviation, most, pieces=(), held_as=jnp.bfloat16):
    values = deviation * jax.random.normal(own_key, extent, jnp.float32)
    if pieces:
        values = values * steps_of(own_key, extent, pieces, -0.22, 0.18)
    return jnp.clip(values, -most, most).astype(held_as)


def setup_inputs(seed: int = 0, part: int = 0) -> dict:
    splits = jax.random.split(jax.random.key(seed), 8)
    part_keys = jax.random.split(jax.random.fold_in(splits[7], part), 8)
    return {
        "output_gradient": normal_values(part_keys[0], (TOKENS, MODEL_DIM), 1.0, 6.0, ((0, 16),)),
        "hidden": normal_values(part_keys[1], (TOKENS, HIDDEN_UNITS), 1.0, 6.0, ((1, 16),)),
        "down_matrix": normal_values(splits[2], (HIDDEN_UNITS, MODEL_DIM), HIDDEN_UNITS ** -0.5, 0.03125, ((0, 16),)),
        "first_adapter_factor": normal_values(part_keys[3], (ADAPTER_COUNT, HIDDEN_UNITS, ADAPTER_RANK), HIDDEN_UNITS ** -0.5, 0.03125, ((1, 16),)),
        "second_adapter_factor": normal_values(part_keys[4], (ADAPTER_COUNT, ADAPTER_RANK, MODEL_DIM), ADAPTER_RANK ** -0.5, 0.75, ((0, 16),)),
        "counts": ragged_sizes(part_keys[5], ADAPTER_COUNT, TOKENS, MAX_TOKENS, 2).astype(jnp.int32),
        "adapter_slots": jax.random.permutation(part_keys[6], ADAPTER_COUNT).astype(jnp.int32),
    }


adapter_scale = 2.0


def token_layout(counts, total_tokens):
    seg_ends = jnp.cumsum(counts).astype(jnp.int32)
    segment_starts = (seg_ends - counts).astype(jnp.int32)
    token_ids = jnp.arange(total_tokens, dtype=jnp.int32)
    token_adapter = jnp.sum((seg_ends[None, :] <= token_ids[:, None]).astype(jnp.int32), axis=1).astype(jnp.int32)
    position_within = (token_ids - segment_starts[token_adapter]).astype(jnp.int32)
    return segment_starts, token_adapter, position_within


def reference(output_gradient, hidden, down_matrix, first_adapter_factor, second_adapter_factor, counts, adapter_slots):
    segment_starts, token_adapter, position_within = token_layout(counts, output_gradient.shape[0])
    slot_range = jnp.arange(MAX_TOKENS, dtype=jnp.int32)
    active_rows = (slot_range[None, :] < counts[:, None]).astype(jnp.float32)
    hidden_pad = jnp.concatenate([hidden, jnp.zeros((MAX_TOKENS, HIDDEN_UNITS), jnp.bfloat16)], axis=0)
    grad_pad = jnp.concatenate([output_gradient, jnp.zeros((MAX_TOKENS, MODEL_DIM), jnp.bfloat16)], axis=0)

    def adapter_wise(inputs):
        first_row, live_mask, first_weights, slot_position = inputs
        hidden_rows = lax.dynamic_slice_in_dim(hidden_pad, first_row, MAX_TOKENS, 0)
        gradient_rows = (lax.dynamic_slice_in_dim(grad_pad, first_row, MAX_TOKENS, 0).astype(jnp.float32) * live_mask[:, None]).astype(jnp.bfloat16)
        low_part = jnp.dot(hidden_rows, first_weights, preferred_element_type=jnp.float32) * live_mask[:, None]
        low_rank_half = low_part.astype(jnp.bfloat16)
        second_gradient = adapter_scale * jnp.dot(low_rank_half.T, gradient_rows, preferred_element_type=jnp.float32)
        second_weights = second_adapter_factor[slot_position]
        backward_rank = jnp.dot(gradient_rows, second_weights.T, preferred_element_type=jnp.float32).astype(jnp.bfloat16)
        adapter_segment = jnp.dot(backward_rank, first_weights.T, preferred_element_type=jnp.float32)
        return second_gradient, adapter_segment

    second_gradients, adapter_segments = lax.map(adapter_wise, (segment_starts, active_rows, first_adapter_factor, adapter_slots))
    second_factor_gradient = jnp.zeros((ADAPTER_COUNT, ADAPTER_RANK, MODEL_DIM), jnp.float32).at[adapter_slots].set(second_gradients)
    dense_gradient = jnp.dot(output_gradient, down_matrix.T, preferred_element_type=jnp.float32)
    selected = adapter_segments.reshape(ADAPTER_COUNT * MAX_TOKENS, HIDDEN_UNITS)[token_adapter * MAX_TOKENS + position_within]
    hidden_gradient = (dense_gradient + adapter_scale * selected).astype(jnp.bfloat16)
    return hidden_gradient, second_factor_gradient
```

```python
import functools

import jax
import jax.numpy as jnp
from jax import lax
from jax.experimental import pallas as pl
from jax.experimental.pallas import tpu as pltpu
from jax.sharding import PartitionSpec as P

MAX_TOKENS = 36


adapter_scale = 2.0


def token_layout(counts, total_tokens):
    seg_ends = jnp.cumsum(counts)
    segment_starts = seg_ends - counts
    token_ids = jnp.arange(total_tokens, dtype=jnp.int32)
    token_adapter = jnp.sum((seg_ends[None, :] <= token_ids[:, None]).astype(jnp.int32), axis=1)
    position_within = token_ids - segment_starts[token_adapter]
    return (segment_starts, token_adapter, position_within)


def per_device_general(
    output_gradient,
    hidden,
    down_matrix,
    first_adapter_factor,
    second_adapter_factor,
    counts,
    adapter_slots,
):
    tok_dev = output_gradient.shape[0]
    devices = lax.axis_size("tensor")
    total_tokens = tok_dev * devices
    segment_width = hidden.shape[1]
    adapter_list = first_adapter_factor.shape[0]
    device_wise = second_adapter_factor.shape[0]
    segment_starts, token_adapter, position_within = token_layout(counts, total_tokens)
    slot_range = jnp.arange(MAX_TOKENS, dtype=jnp.int32)
    active_rows = (slot_range[None, :] < counts[:, None]).astype(jnp.float32)
    hidden_pad = jnp.concatenate(
        [hidden, jnp.zeros((MAX_TOKENS, segment_width), jnp.bfloat16)], axis=0
    )
    index_grid = segment_starts[:, None] + slot_range[None, :]
    hidden_rows = hidden_pad[index_grid]
    low_part = (
        jnp.einsum(
            "heg,hga->hea", hidden_rows, first_adapter_factor, preferred_element_type=jnp.float32
        )
        * active_rows[:, :, None]
    )
    slot_ids = jnp.arange(adapter_list, dtype=jnp.int32)
    holder = jnp.sum(
        jnp.where(adapter_slots[None, :] == slot_ids[:, None], slot_ids[None, :], 0), axis=1
    )
    my_first = lax.axis_index("tensor") * device_wise
    my_adapters = lax.dynamic_slice_in_dim(holder, my_first, device_wise, 0)
    my_starts = segment_starts[my_adapters]
    my_counts = counts[my_adapters]
    my_live = slot_range[None, :] < my_counts[:, None]
    summed = lax.psum(low_part[holder], "tensor")
    own_share = lax.dynamic_slice_in_dim(summed, my_first, device_wise, 0)
    low_rank_half = own_share.astype(jnp.bfloat16)
    target_rows = my_starts[:, None, None] + slot_range[None, :, None]
    shard_rows = lax.all_gather(output_gradient, "tensor", axis=0, tiled=True)
    matrix_product = lax.dot_general(
        shard_rows, down_matrix, (((1,), (1,)), ((), ())), preferred_element_type=jnp.float32
    )
    row_ids = jnp.arange(shard_rows.shape[0], dtype=jnp.int32)
    picker = ((target_rows == row_ids[None, None, :]) & my_live[:, :, None]).astype(jnp.bfloat16)
    own_acc = jnp.einsum("jmr,rd->jmd", picker, shard_rows, preferred_element_type=jnp.float32)
    gradient_rows = own_acc.astype(jnp.bfloat16)
    second_gradient = adapter_scale * jnp.einsum(
        "jmr,jmd->jrd", low_rank_half, gradient_rows, preferred_element_type=jnp.float32
    )
    backward_rank = jnp.einsum(
        "xch,xbh->xcb", gradient_rows, second_adapter_factor, preferred_element_type=jnp.float32
    ).astype(jnp.bfloat16)
    every_back = lax.all_gather(backward_rank, "tensor", axis=0, tiled=True)
    backward_adapter = every_back[adapter_slots]
    adapter_segment = jnp.einsum(
        "yvu,ycu->yvc", backward_adapter, first_adapter_factor, preferred_element_type=jnp.float32
    )
    selected = adapter_segment.reshape(adapter_list * MAX_TOKENS, segment_width)[
        token_adapter * MAX_TOKENS + position_within
    ]
    hidden_gradient = (matrix_product + adapter_scale * selected).astype(jnp.bfloat16)
    return (hidden_gradient, second_gradient)


CHUNKS = 4
HALF_LOW = 24
HALF_BACK = 32
NT = (((1,), (1,)), ((), ()))
NN = (((1,), (0,)), ((), ()))
MESH = pl.DeviceIdType.MESH


def dot(a, b, dims):
    return lax.dot_general(a, b, dims, preferred_element_type=jnp.float32)


def ring_place(chip):
    z, x = chip // 2, chip % 2
    return z + x * (7 - 2 * z)


def ring_chip(place):
    x = place // 4
    z = place + x * (7 - 2 * place)
    return z * 2 + x


def fused_kernel(
    counts,
    slots,
    og,
    second,
    hidden_hbm,
    at_hbm,
    down_hbm,
    out,
    sg,
    gathered,
    rows,
    down,
    at,
    hidden,
    total,
    low_send,
    low_recv,
    back_send,
    back_all,
    wide,
    local_sems,
    ring_send,
    ring_recv,
    sib_send,
    sib_recv,
    low_ssem,
    low_rsem,
    back_ssem,
    back_rsem,
):
    f32, bf16, i32 = jnp.float32, jnp.bfloat16, jnp.int32
    me = lax.axis_index("tensor")
    n = 16
    tokens = rows.shape[0]
    adapters = counts.shape[0]
    width = out.shape[1]
    core, chip = me % 2, me // 2
    place = ring_place(chip)
    sibling = chip * 2 + (1 - core)

    def at_distance(step):
        return ring_chip((place + step + 8) % 8) * 2 + core

    right, left = at_distance(1), at_distance(-1)

    in_copies = [
        pltpu.make_async_copy(hidden_hbm, hidden, local_sems.at[0]),
        pltpu.make_async_copy(at_hbm, at, local_sems.at[1]),
    ]
    span = down.shape[1] // 4
    for b in range(4):
        in_copies.append(
            pltpu.make_async_copy(
                down_hbm.at[:, pl.ds(b * span, span)],
                down.at[:, pl.ds(b * span, span)],
                local_sems.at[2 + b],
            )
        )
    for c in in_copies:
        c.start()

    barrier = pltpu.get_barrier_semaphore()
    for d in range(1, n):
        pl.semaphore_signal(
            barrier, inc=1, device_id={"tensor": (me + d) % n}, device_id_type=MESH
        )

    quarter = og.shape[1] // 4
    step_cols = quarter // CHUNKS
    own = og.shape[0]
    r_out = lax.broadcasted_iota(i32, (4 * own, own), 0)
    r_in = lax.broadcasted_iota(i32, (4 * own, own), 1)
    for c in range(CHUNKS):
        acc = None
        for q in range(4):
            pick = jnp.where(r_out == r_in + q * own, 1.0, 0.0).astype(bf16)
            part = og[:, q * quarter + c * step_cols : q * quarter + (c + 1) * step_cols]
            term = dot(pick, part, NN)
            acc = term if acc is None else acc + term
        gathered[c, me] = acc.astype(bf16)

    pl.semaphore_wait(barrier, n - 1)

    hops = [(4, 3) if c % 2 == 0 else (3, 4) for c in range(CHUNKS)]
    sends = []

    def ring_copy(c, way, hop):
        source = at_distance(-(hop - 1)) if way == 0 else at_distance(hop - 1)
        block = gathered.at[c, source]
        return pltpu.make_async_remote_copy(
            src_ref=block,
            dst_ref=block,
            send_sem=ring_send.at[c, way, hop - 1],
            recv_sem=ring_recv.at[c, way, hop - 1],
            device_id={"tensor": right if way == 0 else left},
            device_id_type=MESH,
        )

    def ring_arrival(c, way, hop):
        source = at_distance(-hop) if way == 0 else at_distance(hop)
        block = gathered.at[c, source]
        return pltpu.make_async_remote_copy(
            src_ref=block,
            dst_ref=block,
            send_sem=ring_send.at[c, way, hop - 1],
            recv_sem=ring_recv.at[c, way, hop - 1],
            device_id={"tensor": right if way == 0 else left},
            device_id_type=MESH,
        )

    def sib_copy(c, kind, source):
        block = gathered.at[c, source]
        return pltpu.make_async_remote_copy(
            src_ref=block,
            dst_ref=block,
            send_sem=sib_send.at[c, kind],
            recv_sem=sib_recv.at[c, kind],
            device_id={"tensor": sibling},
            device_id_type=MESH,
        )

    def other(source):
        return (source // 2) * 2 + (1 - core)

    def start(copy):
        copy.start()
        sends.append(copy)

    for c in range(CHUNKS):
        for way in (0, 1):
            start(ring_copy(c, way, 1))
        start(sib_copy(c, 0, me))

    def layout(shape, axis):
        ids = lax.broadcasted_iota(i32, shape, axis)
        adapter = jnp.zeros(shape, i32)
        slot = jnp.zeros(shape, i32)
        position = jnp.zeros(shape, i32)
        begin = jnp.int32(0)
        for k in range(adapters):
            end = begin + counts[k]
            here = (ids >= begin) & (ids < end)
            adapter = jnp.where(here, k, adapter)
            slot = jnp.where(here, slots[k], slot)
            position = jnp.where(here, ids - begin, position)
            begin = end
        return adapter, slot, position

    adapter_r, slot_r, pos_r = layout((tokens, 128), 0)
    lane_half = lax.broadcasted_iota(i32, (tokens, 128), 1) >= 64
    _, slot_l, pos_l = layout((8, tokens), 1)
    slot_l, pos_l = slot_l[0:1], pos_l[0:1]
    member = adapter_r - jnp.where(lane_half, 1, 0)

    def pick_rows(first, count, half):
        ids = lax.broadcasted_iota(i32, (count, tokens), 0) + first
        high = pos_l >= half
        at_row = slot_l * half + jnp.where(high, pos_l - half, pos_l)
        lo = jnp.where((ids == at_row) & jnp.logical_not(high), 1.0, 0.0).astype(bf16)
        hi = jnp.where((ids == at_row) & high, 1.0, 0.0).astype(bf16)
        return lo, hi

    in_copies[0].wait()
    in_copies[1].wait()
    dup = jnp.zeros((tokens, 128), f32)
    h = hidden[...]
    for g in range(adapters // 4):
        two = dot(h, at[g * 256 : (g + 1) * 256, :], NT)
        for s in range(2):
            dup += jnp.where(member == 4 * g + 2 * s, two[:, s * 128 : (s + 1) * 128], 0.0)
    dup = dup + pltpu.roll(dup, 64, 1)
    top = dup.astype(bf16)
    rest = (dup - top.astype(f32)).astype(bf16)
    lo, hi = pick_rows(0, n * HALF_LOW, HALF_LOW)
    half_out = lax.broadcasted_iota(i32, (n * HALF_LOW, 128), 1) >= 64
    packed = jnp.where(half_out, dot(hi, top, NN) + dot(hi, rest, NN), dot(lo, top, NN) + dot(lo, rest, NN))
    low_send[...] = packed.reshape(n, HALF_LOW, 128)
    low_copies = []
    for d in range(1, n):
        peer = (me + d) % n
        copy = pltpu.make_async_remote_copy(
            src_ref=low_send.at[peer],
            dst_ref=low_recv.at[me],
            send_sem=low_ssem.at[d],
            recv_sem=low_rsem.at[d],
            device_id={"tensor": peer},
            device_id_type=MESH,
        )
        copy.start()
        low_copies.append(copy)

    def hop_step(c, hop):
        for way in (0, 1):
            if hop <= hops[c][way]:
                ring_arrival(c, way, hop).wait_recv()
                if hop < hops[c][way]:
                    start(ring_copy(c, way, hop + 1))
                source = at_distance(-hop) if way == 0 else at_distance(hop)
                start(sib_copy(c, way * 4 + hop, source))

    def sib_wait(c):
        sib_copy(c, 0, sibling).wait_recv()
        for way in (0, 1):
            for hop in range(1, hops[c][way] + 1):
                source = at_distance(-hop) if way == 0 else at_distance(hop)
                sib_copy(c, way * 4 + hop, other(source)).wait_recv()

    for hop in range(1, 4):
        for c in range(CHUNKS):
            hop_step(c, hop)

    for c in in_copies[2:]:
        c.wait()

    four = 16 * own
    p_out = lax.broadcasted_iota(i32, (four, four), 0)
    p_in = lax.broadcasted_iota(i32, (four, four), 1)
    wanted = ((p_out % (4 * own)) // own) * (4 * own) + (p_out // (4 * own)) * own + p_out % own
    order = jnp.where(p_in == wanted, 1.0, 0.0).astype(bf16)

    def unpack(c):
        for g in range(4):
            block = gathered[c, 4 * g : 4 * (g + 1)].reshape(four, step_cols)
            sorted_rows = dot(order, block, NN).astype(bf16)
            for q in range(4):
                col = q * quarter + c * step_cols
                rows[4 * own * g : 4 * own * (g + 1), col : col + step_cols] = sorted_rows[
                    4 * own * q : 4 * own * (q + 1)
                ]

    def matmul(c):
        def tile(first, count):
            acc = None
            for q in range(4):
                col = q * quarter + c * step_cols
                term = dot(
                    rows[:, col : col + step_cols],
                    down[pl.ds(first, count), col : col + step_cols],
                    NT,
                )
                acc = term if acc is None else acc + term
            if c == 0:
                total[:, pl.ds(first, count)] = acc
            else:
                total[:, pl.ds(first, count)] += acc

        def body(i, carry):
            tile(pl.multiple_of(i * 256, 256), 256)
            return carry

        lax.fori_loop(0, width // 256, body, 0)
        tile(width // 256 * 256, width % 256)

    def back_part(c, acc):
        for q in range(4):
            col = q * quarter + c * step_cols
            b = second[:, col : col + step_cols]
            term = dot(rows[:, col : col + step_cols], jnp.concatenate([b, b], axis=0), NT)
            acc = term if acc is None else acc + term
        return acc

    back = None
    hop_step(0, 4)
    for c in range(CHUNKS - 1):
        hop_step(c + 1, 4)
        sib_wait(c)
        unpack(c)
        back = back_part(c, back)
        matmul(c)
    last = CHUNKS - 1
    sib_wait(last)
    unpack(last)
    back = back_part(last, back).astype(bf16)

    lo, hi = pick_rows(me * HALF_BACK, HALF_BACK, HALF_BACK)
    half_out = lax.broadcasted_iota(i32, (HALF_BACK, 128), 1) >= 64
    mine = jnp.where(half_out, dot(hi, back, NN), dot(lo, back, NN)).astype(bf16)
    back_send[...] = mine
    back_copies = []
    for d in range(1, n):
        copy = pltpu.make_async_remote_copy(
            src_ref=back_send,
            dst_ref=back_all.at[me],
            send_sem=back_ssem.at[d],
            recv_sem=back_rsem.at[d],
            device_id={"tensor": (me + d) % n},
            device_id_type=MESH,
        )
        copy.start()
        back_copies.append(copy)
    back_all[me] = mine
    matmul(last)

    low = low_send[me]
    for d in range(1, n):
        source = (me + n - d) % n
        pltpu.make_async_remote_copy(
            src_ref=low_send.at[source],
            dst_ref=low_recv.at[source],
            send_sem=low_ssem.at[d],
            recv_sem=low_rsem.at[d],
            device_id={"tensor": source},
            device_id_type=MESH,
        ).wait_recv()
        low = low + low_recv[source]
    low = 2.0 * low.astype(bf16).astype(f32)
    low_t = jnp.transpose(jnp.concatenate([low, jnp.zeros((128 - HALF_LOW, 128), f32)], axis=0))
    low_t = low_t.astype(bf16)
    lo, hi = pick_rows(me * HALF_LOW, 128, HALF_LOW)
    local_row = lax.broadcasted_iota(i32, (128, tokens), 0) < HALF_LOW
    zero = jnp.zeros_like(lo)
    lo, hi = jnp.where(local_row, lo, zero), jnp.where(local_row, hi, zero)
    low_tok = (dot(low_t[0:64], lo, NN) + dot(low_t[64:128], hi, NN)).astype(bf16)
    for b in range(8):
        cols = pl.ds(b * 1024, 1024)
        sg[:, cols] = dot(low_tok, rows[:, cols], NN)

    for d in range(1, n):
        source = (me + n - d) % n
        pltpu.make_async_remote_copy(
            src_ref=back_send,
            dst_ref=back_all.at[source],
            send_sem=back_ssem.at[d],
            recv_sem=back_rsem.at[d],
            device_id={"tensor": source},
            device_id_type=MESH,
        ).wait_recv()
    count = n * HALF_BACK
    cols = lax.broadcasted_iota(i32, (tokens, count), 1)
    slot_c, pos_c = slot_r[:, 0:1], pos_r[:, 0:1]
    high = pos_c >= HALF_BACK
    at_col = slot_c * HALF_BACK + jnp.where(high, pos_c - HALF_BACK, pos_c)
    hit = cols == at_col
    lo = jnp.where(hit & jnp.logical_not(high), 1.0, 0.0).astype(bf16)
    hi = jnp.where(hit & high, 1.0, 0.0).astype(bf16)
    every = back_all[...].reshape(count, 128)
    z = jnp.where(lane_half, dot(hi, every, NN), dot(lo, every, NN))
    z = 2.0 * (z + pltpu.roll(z, 64, 1))
    for g in range(adapters // 2):
        wide[:, g * 128 : (g + 1) * 128] = jnp.where(member == 2 * g, z, 0.0).astype(bf16)

    def finish(first, count):
        term = dot(wide[...], at[:, pl.ds(first, count)], NN)
        out[:, pl.ds(first, count)] = (total[:, pl.ds(first, count)] + term).astype(bf16)

    def body(i, carry):
        finish(pl.multiple_of(i * 256, 256), 256)
        return carry

    lax.fori_loop(0, width // 256, body, 0)
    finish(width // 256 * 256, width % 256)

    for copy in sends + low_copies + back_copies:
        copy.wait_send()


def per_device_fused(
    output_gradient,
    hidden,
    down_matrix,
    first_adapter_factor,
    second_adapter_factor,
    counts,
    adapter_slots,
):
    bf16, f32 = jnp.bfloat16, jnp.float32
    own, model = output_gradient.shape
    n = lax.axis_size("tensor")
    tokens, width = hidden.shape
    adapters, _, rank = first_adapter_factor.shape
    at = jnp.transpose(first_adapter_factor, (0, 2, 1)).reshape(adapters * rank, width)
    second = second_adapter_factor.reshape(rank, model)
    vmem = pl.BlockSpec(memory_space=pltpu.VMEM)
    smem = pl.BlockSpec(memory_space=pltpu.SMEM)
    hbm = pl.BlockSpec(memory_space=pl.ANY)
    dma = pltpu.SemaphoreType.DMA
    grad, sg = pl.pallas_call(
        fused_kernel,
        out_shape=(
            jax.ShapeDtypeStruct((tokens, width), bf16),
            jax.ShapeDtypeStruct((rank, model), f32),
        ),
        in_specs=[smem, smem, vmem, vmem, hbm, hbm, hbm],
        out_specs=(vmem, vmem),
        scratch_shapes=[
            pltpu.VMEM((CHUNKS, n, 4 * own, model // 4 // CHUNKS), bf16),
            pltpu.VMEM((tokens, model), bf16),
            pltpu.VMEM((width, model), bf16),
            pltpu.VMEM((adapters * rank, width), bf16),
            pltpu.VMEM((tokens, width), bf16),
            pltpu.VMEM((tokens, width), f32),
            pltpu.VMEM((n, HALF_LOW, 128), f32),
            pltpu.VMEM((n, HALF_LOW, 128), f32),
            pltpu.VMEM((HALF_BACK, 128), bf16),
            pltpu.VMEM((n, HALF_BACK, 128), bf16),
            pltpu.VMEM((tokens, adapters * rank), bf16),
            dma((6,)),
            dma((CHUNKS, 2, 4)),
            dma((CHUNKS, 2, 4)),
            dma((CHUNKS, 9)),
            dma((CHUNKS, 9)),
            dma((n,)),
            dma((n,)),
            dma((n,)),
            dma((n,)),
        ],
        compiler_params=pltpu.CompilerParams(
            collective_id=0, has_side_effects=True, vmem_limit_bytes=60 * 1024 * 1024
        ),
        cost_estimate=pl.CostEstimate(
            flops=2 * tokens * width * (model + 2 * adapters * rank),
            bytes_accessed=2 * width * (model + adapters * rank),
            transcendentals=0,
        ),
    )(counts, adapter_slots, output_gradient, second, hidden, at, down_matrix)
    return grad, sg.reshape(1, rank, model)


def per_device(*arrays):
    output_gradient, hidden, _, first_adapter_factor, second_adapter_factor = arrays[:5]
    fits = (
        lax.axis_size("tensor") == 16
        and output_gradient.shape == (12, 8192)
        and hidden.shape[0] == 192
        and first_adapter_factor.shape[0] == 16
        and first_adapter_factor.shape[2] == 64
        and second_adapter_factor.shape[0] == 1
    )
    return (per_device_fused if fits else per_device_general)(*arrays)


def solution(mesh):
    placed = (
        P(("groups", "tensor"), None),
        P("groups", "tensor"),
        P("tensor", None),
        P("groups", "tensor", None),
        P(("groups", "tensor"), None, None),
        P("groups"),
        P("groups"),
    )
    return jax.shard_map(
        per_device,
        mesh=mesh,
        in_specs=placed,
        out_specs=(P("groups", "tensor"), P(("groups", "tensor"), None, None)),
        check_vma=False,
    )
```

```python
import functools

import jax
import jax.numpy as jnp
from jax import lax
from jax.experimental import pallas as pl
from jax.experimental.pallas import tpu as pltpu
from jax.sharding import PartitionSpec as P

MAX_TOKENS = 36


adapter_scale = 2.0


def token_layout(counts, total_tokens):
    seg_ends = jnp.cumsum(counts)
    segment_starts = seg_ends - counts
    token_ids = jnp.arange(total_tokens, dtype=jnp.int32)
    token_adapter = jnp.sum((seg_ends[None, :] <= token_ids[:, None]).astype(jnp.int32), axis=1)
    position_within = token_ids - segment_starts[token_adapter]
    return (segment_starts, token_adapter, position_within)


def per_device_general(
    output_gradient,
    hidden,
    down_matrix,
    first_adapter_factor,
    second_adapter_factor,
    counts,
    adapter_slots,
):
    tok_dev = output_gradient.shape[0]
    devices = lax.axis_size("tensor")
    total_tokens = tok_dev * devices
    segment_width = hidden.shape[1]
    adapter_list = first_adapter_factor.shape[0]
    device_wise = second_adapter_factor.shape[0]
    segment_starts, token_adapter, position_within = token_layout(counts, total_tokens)
    slot_range = jnp.arange(MAX_TOKENS, dtype=jnp.int32)
    active_rows = (slot_range[None, :] < counts[:, None]).astype(jnp.float32)
    hidden_pad = jnp.concatenate(
        [hidden, jnp.zeros((MAX_TOKENS, segment_width), jnp.bfloat16)], axis=0
    )
    index_grid = segment_starts[:, None] + slot_range[None, :]
    hidden_rows = hidden_pad[index_grid]
    low_part = (
        jnp.einsum(
            "heg,hga->hea", hidden_rows, first_adapter_factor, preferred_element_type=jnp.float32
        )
        * active_rows[:, :, None]
    )
    slot_ids = jnp.arange(adapter_list, dtype=jnp.int32)
    holder = jnp.sum(
        jnp.where(adapter_slots[None, :] == slot_ids[:, None], slot_ids[None, :], 0), axis=1
    )
    my_first = lax.axis_index("tensor") * device_wise
    my_adapters = lax.dynamic_slice_in_dim(holder, my_first, device_wise, 0)
    my_starts = segment_starts[my_adapters]
    my_counts = counts[my_adapters]
    my_live = slot_range[None, :] < my_counts[:, None]
    summed = lax.psum(low_part[holder], "tensor")
    own_share = lax.dynamic_slice_in_dim(summed, my_first, device_wise, 0)
    low_rank_half = own_share.astype(jnp.bfloat16)
    target_rows = my_starts[:, None, None] + slot_range[None, :, None]
    shard_rows = lax.all_gather(output_gradient, "tensor", axis=0, tiled=True)
    matrix_product = lax.dot_general(
        shard_rows, down_matrix, (((1,), (1,)), ((), ())), preferred_element_type=jnp.float32
    )
    row_ids = jnp.arange(shard_rows.shape[0], dtype=jnp.int32)
    picker = ((target_rows == row_ids[None, None, :]) & my_live[:, :, None]).astype(jnp.bfloat16)
    own_acc = jnp.einsum("jmr,rd->jmd", picker, shard_rows, preferred_element_type=jnp.float32)
    gradient_rows = own_acc.astype(jnp.bfloat16)
    second_gradient = adapter_scale * jnp.einsum(
        "jmr,jmd->jrd", low_rank_half, gradient_rows, preferred_element_type=jnp.float32
    )
    backward_rank = jnp.einsum(
        "xch,xbh->xcb", gradient_rows, second_adapter_factor, preferred_element_type=jnp.float32
    ).astype(jnp.bfloat16)
    every_back = lax.all_gather(backward_rank, "tensor", axis=0, tiled=True)
    backward_adapter = every_back[adapter_slots]
    adapter_segment = jnp.einsum(
        "yvu,ycu->yvc", backward_adapter, first_adapter_factor, preferred_element_type=jnp.float32
    )
    selected = adapter_segment.reshape(adapter_list * MAX_TOKENS, segment_width)[
        token_adapter * MAX_TOKENS + position_within
    ]
    hidden_gradient = (matrix_product + adapter_scale * selected).astype(jnp.bfloat16)
    return (hidden_gradient, second_gradient)


CHUNKS = 4
HALF_LOW = 24
HALF_BACK = 32
NT = (((1,), (1,)), ((), ()))
NN = (((1,), (0,)), ((), ()))
MESH = pl.DeviceIdType.MESH


def dot(a, b, dims):
    return lax.dot_general(a, b, dims, preferred_element_type=jnp.float32)


def ring_place(chip):
    z, x = chip // 2, chip % 2
    return z + x * (7 - 2 * z)


def ring_chip(place):
    x = place // 4
    z = place + x * (7 - 2 * place)
    return z * 2 + x


def fused_kernel(
    counts,
    slots,
    og,
    second,
    hidden_hbm,
    at_hbm,
    down_hbm,
    out,
    sg,
    gathered,
    rows,
    down,
    at,
    hidden,
    total,
    low_send,
    low_recv,
    back_send,
    back_all,
    wide,
    local_sems,
    ring_send,
    ring_recv,
    sib_send,
    sib_recv,
    low_ssem,
    low_rsem,
    back_ssem,
    back_rsem,
):
    f32, bf16, i32 = jnp.float32, jnp.bfloat16, jnp.int32
    me = lax.axis_index("tensor")
    n = 16
    tokens = rows.shape[0]
    adapters = counts.shape[0]
    width = out.shape[1]
    core, chip = me % 2, me // 2
    place = ring_place(chip)
    sibling = chip * 2 + (1 - core)

    def at_distance(step):
        return ring_chip((place + step + 8) % 8) * 2 + core

    right, left = at_distance(1), at_distance(-1)

    in_copies = [
        pltpu.make_async_copy(hidden_hbm, hidden, local_sems.at[0]),
        pltpu.make_async_copy(at_hbm, at, local_sems.at[1]),
    ]
    span = down.shape[1] // 4
    for b in range(4):
        in_copies.append(
            pltpu.make_async_copy(
                down_hbm.at[:, pl.ds(b * span, span)],
                down.at[:, pl.ds(b * span, span)],
                local_sems.at[2 + b],
            )
        )
    for c in in_copies:
        c.start()

    barrier = pltpu.get_barrier_semaphore()
    for d in range(1, n):
        pl.semaphore_signal(
            barrier, inc=1, device_id={"tensor": (me + d) % n}, device_id_type=MESH
        )

    quarter = og.shape[1] // 4
    step_cols = quarter // CHUNKS
    own = og.shape[0]
    r_out = lax.broadcasted_iota(i32, (4 * own, own), 0)
    r_in = lax.broadcasted_iota(i32, (4 * own, own), 1)
    for c in range(CHUNKS):
        acc = None
        for q in range(4):
            pick = jnp.where(r_out == r_in + q * own, 1.0, 0.0).astype(bf16)
            part = og[:, q * quarter + c * step_cols : q * quarter + (c + 1) * step_cols]
            term = dot(pick, part, NN)
            acc = term if acc is None else acc + term
        gathered[c, me] = acc.astype(bf16)

    pl.semaphore_wait(barrier, n - 1)

    hops = [(4, 3) if c % 2 == 0 else (3, 4) for c in range(CHUNKS)]
    sends = []

    def ring_copy(c, way, hop):
        source = at_distance(-(hop - 1)) if way == 0 else at_distance(hop - 1)
        block = gathered.at[c, source]
        return pltpu.make_async_remote_copy(
            src_ref=block,
            dst_ref=block,
            send_sem=ring_send.at[c, way, hop - 1],
            recv_sem=ring_recv.at[c, way, hop - 1],
            device_id={"tensor": right if way == 0 else left},
            device_id_type=MESH,
        )

    def ring_arrival(c, way, hop):
        source = at_distance(-hop) if way == 0 else at_distance(hop)
        block = gathered.at[c, source]
        return pltpu.make_async_remote_copy(
            src_ref=block,
            dst_ref=block,
            send_sem=ring_send.at[c, way, hop - 1],
            recv_sem=ring_recv.at[c, way, hop - 1],
            device_id={"tensor": right if way == 0 else left},
            device_id_type=MESH,
        )

    def sib_copy(c, kind, source):
        block = gathered.at[c, source]
        return pltpu.make_async_remote_copy(
            src_ref=block,
            dst_ref=block,
            send_sem=sib_send.at[c, kind],
            recv_sem=sib_recv.at[c, kind],
            device_id={"tensor": sibling},
            device_id_type=MESH,
        )

    def other(source):
        return (source // 2) * 2 + (1 - core)

    def start(copy):
        copy.start()
        sends.append(copy)

    for c in range(CHUNKS):
        for way in (0, 1):
            start(ring_copy(c, way, 1))
        start(sib_copy(c, 0, me))

    def layout(shape, axis):
        ids = lax.broadcasted_iota(i32, shape, axis)
        adapter = jnp.zeros(shape, i32)
        slot = jnp.zeros(shape, i32)
        position = jnp.zeros(shape, i32)
        begin = jnp.int32(0)
        for k in range(adapters):
            end = begin + counts[k]
            here = (ids >= begin) & (ids < end)
            adapter = jnp.where(here, k, adapter)
            slot = jnp.where(here, slots[k], slot)
            position = jnp.where(here, ids - begin, position)
            begin = end
        return adapter, slot, position

    adapter_r, slot_r, pos_r = layout((tokens, 128), 0)
    lane_half = lax.broadcasted_iota(i32, (tokens, 128), 1) >= 64
    _, slot_l, pos_l = layout((8, tokens), 1)
    slot_l, pos_l = slot_l[0:1], pos_l[0:1]
    member = adapter_r - jnp.where(lane_half, 1, 0)

    def pick_rows(first, count, half):
        ids = lax.broadcasted_iota(i32, (count, tokens), 0) + first
        high = pos_l >= half
        at_row = slot_l * half + jnp.where(high, pos_l - half, pos_l)
        lo = jnp.where((ids == at_row) & jnp.logical_not(high), 1.0, 0.0).astype(bf16)
        hi = jnp.where((ids == at_row) & high, 1.0, 0.0).astype(bf16)
        return lo, hi

    in_copies[0].wait()
    in_copies[1].wait()
    dup = jnp.zeros((tokens, 128), f32)
    h = hidden[...]
    for g in range(adapters // 4):
        two = dot(h, at[g * 256 : (g + 1) * 256, :], NT)
        for s in range(2):
            dup += jnp.where(member == 4 * g + 2 * s, two[:, s * 128 : (s + 1) * 128], 0.0)
    dup = dup + pltpu.roll(dup, 64, 1)
    top = dup.astype(bf16)
    rest = (dup - top.astype(f32)).astype(bf16)
    lo, hi = pick_rows(0, n * HALF_LOW, HALF_LOW)
    half_out = lax.broadcasted_iota(i32, (n * HALF_LOW, 128), 1) >= 64
    packed = jnp.where(half_out, dot(hi, top, NN) + dot(hi, rest, NN), dot(lo, top, NN) + dot(lo, rest, NN))
    low_send[...] = packed.reshape(n, HALF_LOW, 128)
    low_copies = []
    for d in range(1, n):
        peer = (me + d) % n
        copy = pltpu.make_async_remote_copy(
            src_ref=low_send.at[peer],
            dst_ref=low_recv.at[me],
            send_sem=low_ssem.at[d],
            recv_sem=low_rsem.at[d],
            device_id={"tensor": peer},
            device_id_type=MESH,
        )
        low_copies.append(copy)

    def hop_step(c, hop):
        for way in (0, 1):
            if hop <= hops[c][way]:
                ring_arrival(c, way, hop).wait_recv()
                if hop < hops[c][way]:
                    start(ring_copy(c, way, hop + 1))
                source = at_distance(-hop) if way == 0 else at_distance(hop)
                start(sib_copy(c, way * 4 + hop, source))

    def sib_wait(c):
        sib_copy(c, 0, sibling).wait_recv()
        for way in (0, 1):
            for hop in range(1, hops[c][way] + 1):
                source = at_distance(-hop) if way == 0 else at_distance(hop)
                sib_copy(c, way * 4 + hop, other(source)).wait_recv()

    for hop in range(1, 4):
        for c in range(CHUNKS):
            hop_step(c, hop)

    for c in in_copies[2:]:
        c.wait()

    four = 16 * own
    p_out = lax.broadcasted_iota(i32, (four, four), 0)
    p_in = lax.broadcasted_iota(i32, (four, four), 1)
    wanted = ((p_out % (4 * own)) // own) * (4 * own) + (p_out // (4 * own)) * own + p_out % own
    order = jnp.where(p_in == wanted, 1.0, 0.0).astype(bf16)

    def unpack(c):
        for g in range(4):
            block = gathered[c, 4 * g : 4 * (g + 1)].reshape(four, step_cols)
            sorted_rows = dot(order, block, NN).astype(bf16)
            for q in range(4):
                col = q * quarter + c * step_cols
                rows[4 * own * g : 4 * own * (g + 1), col : col + step_cols] = sorted_rows[
                    4 * own * q : 4 * own * (q + 1)
                ]

    def matmul(c):
        split = width // 32 * 16 + 16
        for first, count in ((0, split), (split, width - split)):
            acc = None
            for q in range(4):
                col = q * quarter + c * step_cols
                term = dot(
                    down[first : first + count, col : col + step_cols],
                    rows[:, col : col + step_cols],
                    NT,
                )
                acc = term if acc is None else acc + term
            if c == 0:
                total[first : first + count, :] = acc
            else:
                total[first : first + count, :] += acc

    def back_part(c, acc):
        for q in range(4):
            col = q * quarter + c * step_cols
            b = second[:, col : col + step_cols]
            term = dot(rows[:, col : col + step_cols], jnp.concatenate([b, b], axis=0), NT)
            acc = term if acc is None else acc + term
        return acc

    back = None
    hop_step(0, 4)
    for c in range(CHUNKS - 1):
        hop_step(c + 1, 4)
        if c == CHUNKS - 2:
            for copy in low_copies:
                copy.start()
        sib_wait(c)
        unpack(c)
        back = back_part(c, back)
        matmul(c)
    last = CHUNKS - 1
    sib_wait(last)
    unpack(last)
    back = back_part(last, back).astype(bf16)

    lo, hi = pick_rows(me * HALF_BACK, HALF_BACK, HALF_BACK)
    half_out = lax.broadcasted_iota(i32, (HALF_BACK, 128), 1) >= 64
    mine = jnp.where(half_out, dot(hi, back, NN), dot(lo, back, NN)).astype(bf16)
    back_send[...] = mine
    back_copies = []
    for d in range(1, n):
        copy = pltpu.make_async_remote_copy(
            src_ref=back_send,
            dst_ref=back_all.at[me],
            send_sem=back_ssem.at[d],
            recv_sem=back_rsem.at[d],
            device_id={"tensor": (me + d) % n},
            device_id_type=MESH,
        )
        copy.start()
        back_copies.append(copy)
    back_all[me] = mine
    matmul(last)

    low = low_send[me]
    for d in range(1, n):
        source = (me + n - d) % n
        pltpu.make_async_remote_copy(
            src_ref=low_send.at[source],
            dst_ref=low_recv.at[source],
            send_sem=low_ssem.at[d],
            recv_sem=low_rsem.at[d],
            device_id={"tensor": source},
            device_id_type=MESH,
        ).wait_recv()
        low = low + low_recv[source]
    low = 2.0 * low.astype(bf16).astype(f32)
    low_t = jnp.transpose(jnp.concatenate([low, jnp.zeros((128 - HALF_LOW, 128), f32)], axis=0))
    low_t = low_t.astype(bf16)
    lo, hi = pick_rows(me * HALF_LOW, 128, HALF_LOW)
    local_row = lax.broadcasted_iota(i32, (128, tokens), 0) < HALF_LOW
    zero = jnp.zeros_like(lo)
    lo, hi = jnp.where(local_row, lo, zero), jnp.where(local_row, hi, zero)
    low_tok = (dot(low_t[0:64], lo, NN) + dot(low_t[64:128], hi, NN)).astype(bf16)
    for b in range(8):
        cols = pl.ds(b * 1024, 1024)
        sg[:, cols] = dot(low_tok, rows[:, cols], NN)

    for d in range(1, n):
        source = (me + n - d) % n
        pltpu.make_async_remote_copy(
            src_ref=back_send,
            dst_ref=back_all.at[source],
            send_sem=back_ssem.at[d],
            recv_sem=back_rsem.at[d],
            device_id={"tensor": source},
            device_id_type=MESH,
        ).wait_recv()
    count = n * HALF_BACK
    cols = lax.broadcasted_iota(i32, (tokens, count), 1)
    slot_c, pos_c = slot_r[:, 0:1], pos_r[:, 0:1]
    high = pos_c >= HALF_BACK
    at_col = slot_c * HALF_BACK + jnp.where(high, pos_c - HALF_BACK, pos_c)
    hit = cols == at_col
    lo = jnp.where(hit & jnp.logical_not(high), 1.0, 0.0).astype(bf16)
    hi = jnp.where(hit & high, 1.0, 0.0).astype(bf16)
    every = back_all[...].reshape(count, 128)
    z = jnp.where(lane_half, dot(hi, every, NN), dot(lo, every, NN))
    z = 2.0 * (z + pltpu.roll(z, 64, 1))
    for g in range(adapters // 2):
        wide[:, g * 128 : (g + 1) * 128] = jnp.where(member == 2 * g, z, 0.0).astype(bf16)

    def finish(first, count):
        term = dot(wide[...], at[:, pl.ds(first, count)], NN)
        out[:, pl.ds(first, count)] = (jnp.transpose(total[pl.ds(first, count), :]) + term).astype(bf16)

    def body(i, carry):
        finish(pl.multiple_of(i * 256, 256), 256)
        return carry

    lax.fori_loop(0, width // 256, body, 0)
    finish(width // 256 * 256, width % 256)

    for copy in sends + low_copies + back_copies:
        copy.wait_send()


def per_device_fused(
    output_gradient,
    hidden,
    down_matrix,
    first_adapter_factor,
    second_adapter_factor,
    counts,
    adapter_slots,
):
    bf16, f32 = jnp.bfloat16, jnp.float32
    own, model = output_gradient.shape
    n = lax.axis_size("tensor")
    tokens, width = hidden.shape
    adapters, _, rank = first_adapter_factor.shape
    at = jnp.transpose(first_adapter_factor, (0, 2, 1)).reshape(adapters * rank, width)
    second = second_adapter_factor.reshape(rank, model)
    vmem = pl.BlockSpec(memory_space=pltpu.VMEM)
    smem = pl.BlockSpec(memory_space=pltpu.SMEM)
    hbm = pl.BlockSpec(memory_space=pl.ANY)
    dma = pltpu.SemaphoreType.DMA
    grad, sg = pl.pallas_call(
        fused_kernel,
        out_shape=(
            jax.ShapeDtypeStruct((tokens, width), bf16),
            jax.ShapeDtypeStruct((rank, model), f32),
        ),
        in_specs=[smem, smem, vmem, vmem, hbm, hbm, hbm],
        out_specs=(vmem, vmem),
        scratch_shapes=[
            pltpu.VMEM((CHUNKS, n, 4 * own, model // 4 // CHUNKS), bf16),
            pltpu.VMEM((tokens, model), bf16),
            pltpu.VMEM((width, model), bf16),
            pltpu.VMEM((adapters * rank, width), bf16),
            pltpu.VMEM((tokens, width), bf16),
            pltpu.VMEM((width, tokens), f32),
            pltpu.VMEM((n, HALF_LOW, 128), f32),
            pltpu.VMEM((n, HALF_LOW, 128), f32),
            pltpu.VMEM((HALF_BACK, 128), bf16),
            pltpu.VMEM((n, HALF_BACK, 128), bf16),
            pltpu.VMEM((tokens, adapters * rank), bf16),
            dma((6,)),
            dma((CHUNKS, 2, 4)),
            dma((CHUNKS, 2, 4)),
            dma((CHUNKS, 9)),
            dma((CHUNKS, 9)),
            dma((n,)),
            dma((n,)),
            dma((n,)),
            dma((n,)),
        ],
        compiler_params=pltpu.CompilerParams(
            collective_id=0, has_side_effects=True, vmem_limit_bytes=60 * 1024 * 1024
        ),
        cost_estimate=pl.CostEstimate(
            flops=2 * tokens * width * (model + 2 * adapters * rank),
            bytes_accessed=2 * width * (model + adapters * rank),
            transcendentals=0,
        ),
    )(counts, adapter_slots, output_gradient, second, hidden, at, down_matrix)
    return grad, sg.reshape(1, rank, model)


def per_device(*arrays):
    output_gradient, hidden, _, first_adapter_factor, second_adapter_factor = arrays[:5]
    fits = (
        lax.axis_size("tensor") == 16
        and output_gradient.shape == (12, 8192)
        and hidden.shape[0] == 192
        and first_adapter_factor.shape[0] == 16
        and first_adapter_factor.shape[2] == 64
        and second_adapter_factor.shape[0] == 1
    )
    return (per_device_fused if fits else per_device_general)(*arrays)


def solution(mesh):
    placed = (
        P(("groups", "tensor"), None),
        P("groups", "tensor"),
        P("tensor", None),
        P("groups", "tensor", None),
        P(("groups", "tensor"), None, None),
        P("groups"),
        P("groups"),
    )
    return jax.shard_map(
        per_device,
        mesh=mesh,
        in_specs=placed,
        out_specs=(P("groups", "tensor"), P(("groups", "tensor"), None, None)),
        check_vma=False,
    )
```
